32 devices in a mesh: ens: 2 (over x), gx: 16 (over z, y, core).
Axes of the slice: x: 2, y: 2, z: 4, core: 2. Of those that a mesh axis runs over, the one named last changes fastest.
Arguments:
- state: float32 [2, 512, 32, 256], P(None, ('ens', 'gx')), parts along dimension 1, may hold values from -3 to 3
- fine_state: float32 [2, 64, 32, 1024], P(None, ('ens', 'gx')), parts along dimension 1, may hold values from -3 to 3
- box_list: int32 [64, 3], P('ens'), parts along dimension 0, may hold values from 0 to 240, as said below
- plan: int32 [64], P('ens'), parts along dimension 0, may hold values from 0 to 31, as said below
Outputs:
- coarse_out: float32 [2, 512, 32, 256], P(None, ('ens', 'gx')), parts along dimension 1
- fine_out: float32 [2, 64, 32, 1024], P(None, ('ens', 'gx')), parts along dimension 1
The draws below stay inside these ranges and needn't reach their ends.
There are 2 independent parts, one for each index of `ens`. The reference program is written for one: setup_inputs(seed, part) draws one part's arguments, and reference() takes and returns one part's arrays. A program takes and returns all parts, laid end to end along the dimension named above; each array names one. Nothing has to cross between parts.
Inputs may be any that keep to these rules, and one draw needn't show every extreme that they name: `box_list`: every corner coordinate is a multiple of 16 within the grid; boxes do not intersect. plan is a permutation of the box numbers; the box in a slot of device d along gx (slot // 2 == d) has its x corner on device d or on device d - 1 cyclically (x corner // 16).
All inputs are finite; a program needn't handle non-finite values.
Results may differ from the reference program's by a relative error of at most 0.0003.
Values sent between devices are 32-bit elements; how exact they have to be, the bound alone decides.
A program may use at most 128 MiB of HBM per device.

```python
import jax
import jax.numpy as jnp
from jax import lax

FB = 32
CX = 16
NY = 32
NZ = 256
BOX_DEV = 2
NX = 256
NBOX = 32
N_GX = 16


def rotate_first(row, target, places):
    return (row + (target - row[0])) % places


def shared_boxes(key):
    half = FB // 2
    per_y = NY // half
    per_z = NZ // half
    places = CX // half * per_y * per_z
    lag = jax.random.randint(jax.random.fold_in(key, 11), (N_GX, BOX_DEV), 0, 2)
    lag = lag.at[0, 0].set(0).at[N_GX - 1, 0].set(0)
    owner = (jnp.arange(N_GX, dtype=jnp.int32)[:, None] - lag) % N_GX
    row_keys = jax.random.split(jax.random.fold_in(key, 12), N_GX)
    orders = jax.vmap(lambda single: jax.random.permutation(single, places))(row_keys).astype(jnp.int32)
    orders = orders.at[0].set(rotate_first(orders[0], 0, places))
    orders = orders.at[N_GX - 1].set(rotate_first(orders[N_GX - 1], places - 1, places))
    column = lag * BOX_DEV + jnp.arange(BOX_DEV, dtype=jnp.int32)[None, :]
    place = orders[owner, column]
    corner_x = owner * CX + place // (per_y * per_z) * half
    corner_y = place // per_z % per_y * half
    corner_z = place % per_z * half
    by_slot = jnp.stack([corner_x, corner_y, corner_z], axis=-1).reshape(N_GX * BOX_DEV, 3).astype(jnp.int32)
    shuffle = jax.random.permutation(jax.random.fold_in(key, 13), N_GX * BOX_DEV).astype(jnp.int32)
    listing = jnp.zeros((N_GX * BOX_DEV, 3), jnp.int32).at[shuffle].set(by_slot)
    return (listing, shuffle)


def draw_box_list(key, part):
    listing, shuffle = shared_boxes(key)
    return listing


def draw_plan(key, part):
    listing, shuffle = shared_boxes(key)
    return shuffle


def levels(key, dims, cuts, low, high):
    loudness, own = 1.0, jax.random.fold_in(key, 6)
    for dim, shards_of in cuts:
        draws = jnp.exp(jax.random.uniform(jax.random.fold_in(own, dim), (shards_of,), jnp.float32, low / len(cuts), high / len(cuts)))
        loudness = loudness * jnp.repeat(draws, dims[dim] // shards_of).reshape([-1 if axis == dim else 1 for axis in range(len(dims))])
    return loudness


def scatter_about(rng, dims, width, reach, cuts=(), held_as=jnp.bfloat16):
    array = jax.random.normal(rng, dims, jnp.float32) * width
    if len(cuts) > 0:
        array = levels(rng, dims, cuts, -0.22, 0.18) * array
    return jnp.clip(array, min=-reach, max=reach).astype(held_as)


def setup_inputs(seed: int = 0, part: int = 0) -> dict:
    keys = jax.random.split(jax.random.key(seed), 5)
    part_splits = jax.random.split(jax.random.fold_in(keys[4], part), 5)
    return {
        "state": scatter_about(part_splits[0], (2, NX, NY, NZ), 0.5, 3.0, ((1, 16),), jnp.float32),
        "fine_state": scatter_about(part_splits[1], (2, NBOX, FB, FB * FB), 0.5, 3.0, ((1, 16),), jnp.float32),
        "box_list": draw_box_list(jax.random.fold_in(jax.random.fold_in(keys[4], part), 71), part),
        "plan": draw_plan(jax.random.fold_in(jax.random.fold_in(keys[4], part), 71), part),
    }


def coarse_force(state):
    displace = state[0]
    centre = displace
    along_x = -jnp.roll(centre, -2, 0) + 16.0 * jnp.roll(centre, -1, 0) - 30.0 * centre + 16.0 * jnp.roll(centre, 1, 0) - jnp.roll(centre, 2, 0)
    along_y = -jnp.roll(centre, -2, 1) + 16.0 * jnp.roll(centre, -1, 1) - 30.0 * centre + 16.0 * jnp.roll(centre, 1, 1) - jnp.roll(centre, 2, 1)
    along_z = -jnp.roll(centre, -2, 2) + 16.0 * jnp.roll(centre, -1, 2) - 30.0 * centre + 16.0 * jnp.roll(centre, 1, 2) - jnp.roll(centre, 2, 2)
    laplace = (along_x + along_y + along_z) / 12.0
    return jnp.stack([state[1], laplace - centre + centre * centre * centre])


def fine_force(dressed):
    displace = dressed[0]
    centre = displace[2:-2, 2:-2, 2:-2]
    along_x = -displace[4:, 2:-2, 2:-2] + 16.0 * displace[3:-1, 2:-2, 2:-2] - 30.0 * centre + 16.0 * displace[1:-3, 2:-2, 2:-2] - displace[:-4, 2:-2, 2:-2]
    along_y = -displace[2:-2, 4:, 2:-2] + 16.0 * displace[2:-2, 3:-1, 2:-2] - 30.0 * centre + 16.0 * displace[2:-2, 1:-3, 2:-2] - displace[2:-2, :-4, 2:-2]
    along_z = -displace[2:-2, 2:-2, 4:] + 16.0 * displace[2:-2, 2:-2, 3:-1] - 30.0 * centre + 16.0 * displace[2:-2, 2:-2, 1:-3] - displace[2:-2, 2:-2, :-4]
    laplace = (along_x + along_y + along_z) / 12.0 * 4.0
    return jnp.stack([dressed[1, 2:-2, 2:-2, 2:-2], laplace - centre + centre * centre * centre])


def fine_run(interior, coarse_old, coarse_new):
    def dress(inner, fraction):
        blend = coarse_old + fraction * (coarse_new - coarse_old)
        upper = jnp.repeat(jnp.repeat(jnp.repeat(blend, 2, 1), 2, 2), 2, 3)
        return upper.at[:, 2:-2, 2:-2, 2:-2].set(inner)
    fine_step = 0.25
    current = interior
    for substep in range(2):
        start = substep * 0.5
        slope_one = fine_force(dress(current, start))
        slope_two = fine_force(dress(current + (fine_step / 2) * slope_one, start + 0.25))
        slope_three = fine_force(dress(current + (fine_step / 2) * slope_two, start + 0.25))
        slope_four = fine_force(dress(current + fine_step * slope_three, start + 0.5))
        current = current + (fine_step / 6.0) * (slope_one + 2.0 * slope_two + 2.0 * slope_three + slope_four)
    return current


def box_means(fine_box):
    half = FB // 2
    return jnp.sum(fine_box.reshape(2, half, 2, half, 2, half, 2), axis=(2, 4, 6)) * 0.125


def reference(state, fine_state, box_list, plan):
    half = FB // 2
    coarse_step = 0.5
    slope_one = coarse_force(state)
    slope_two = coarse_force(state + (coarse_step / 2) * slope_one)
    slope_three = coarse_force(state + (coarse_step / 2) * slope_two)
    slope_four = coarse_force(state + coarse_step * slope_three)
    advanced = state + (coarse_step / 6.0) * (slope_one + 2.0 * slope_two + 2.0 * slope_three + slope_four)
    span = jnp.arange(half + 2, dtype=jnp.int32) - 1

    def patch(grid, corner):
        xs = (corner[0] + span) % NX
        ys = (corner[1] + span) % NY
        zs = (corner[2] + span) % NZ
        return jnp.take(jnp.take(jnp.take(grid, xs, axis=1), ys, axis=2), zs, axis=3)

    def one_slot(slot):
        corner = box_list[plan[slot]]
        interior = fine_state[:, slot].reshape(2, FB, FB, FB)
        return fine_run(interior, patch(state, corner), patch(advanced, corner))

    finished = lax.map(one_slot, jnp.arange(NBOX, dtype=jnp.int32))
    fine_out = jnp.transpose(finished, (1, 0, 2, 3, 4)).reshape(2, NBOX, FB, FB * FB)

    def insert(slot, grid):
        corner = box_list[plan[slot]]
        means = box_means(finished[slot])
        zero = jnp.zeros((), jnp.int32)
        return lax.dynamic_update_slice(grid, means, (zero, corner[0].astype(jnp.int32), corner[1].astype(jnp.int32), corner[2].astype(jnp.int32)))

    coarse_out = lax.fori_loop(0, NBOX, insert, advanced)
    return coarse_out, fine_out
```

```python
import jax
import jax.numpy as jnp
from jax import lax
from jax.experimental import pallas as pl
from jax.experimental.pallas import tpu as pltpu
from jax.sharding import PartitionSpec as P

FB = 32
BOX_DEV = 2
MESH = pl.DeviceIdType.MESH
BF = jnp.bfloat16
F32 = jnp.float32


def iota(shape, dim):
    return lax.broadcasted_iota(jnp.int32, shape, dim)


def halves(a):
    hi = a.astype(BF)
    lo = (a - hi.astype(F32)).astype(BF)
    return hi, lo


def mm(a, b):
    return jnp.dot(a, b, preferred_element_type=F32)


def mm_nt(a, b):
    return lax.dot_general(a, b, (((1,), (1,)), ((), ())), preferred_element_type=F32)


def star(d):
    d = jnp.abs(d)
    return jnp.where(d == 1, 16.0, jnp.where(d == 2, -1.0, 0.0))


def edge(side, j):
    d = jnp.where(side == 0, j, 31 - j)
    return jnp.where(d == 0, 15.0, jnp.where(d == 1, -1.0, 0.0))


def coarse_weights():
    k, j = iota((256, 256), 0), iota((256, 256), 1)
    d = (j - k) & 255
    d = jnp.minimum(d, 256 - d)
    return star(d).astype(BF)


def fine_weights():
    k, j = iota((256, 256), 0), iota((256, 256), 1)
    jy, jz = j >> 5, j & 31
    ky, kz = k >> 5, k & 31
    inner = jnp.where(ky == jy, star(kz - jz), 0.0) + jnp.where(kz == jz, star(ky - jy), 0.0)
    far = jnp.where(k < 128, ky - 4, ky + 4)
    outer = jnp.where(kz == jz, star(far - jy), 0.0)
    return inner.astype(BF), outer.astype(BF)


def boundary_weights():
    k, j = iota((128, 1024), 0), iota((128, 1024), 1)
    y, z = j >> 5, j & 31
    wy = jnp.where((k & 15) == (z >> 1), edge(k >> 6, y), 0.0).astype(BF)
    wzl = jnp.where((k & 31) == (y >> 1), edge(0, z), 0.0).astype(BF)
    wzh = jnp.where((k & 31) == (y >> 1), edge(1, z), 0.0).astype(BF)
    wx = jnp.where((k & 15) == (z >> 1), 1.0, 0.0).astype(BF)
    return wy, wzl, wzh, wx


def mean_weights():
    k, j = iota((1024, 256), 0), iota((1024, 256), 1)
    return jnp.where(((k >> 6) == (j >> 4)) & (((k & 31) >> 1) == (j & 15)), 1.0, 0.0).astype(BF)


def roll(a, shift, axis):
    return pltpu.roll(a, shift % a.shape[axis], axis)


def kernel(
    devices,
    state, fine, boxes, plan,
    coarse_out, fine_out,
    fe, pe, f2, f3, f4, k1, k2, nf, npm,
    q, pad, faces, faces_in, sides, sides_in, means, means_in, cz, fw, bw, mw,
    local_sem, send_sem, recv_sem,
):
    me = lax.axis_index("gx")
    right, left = lax.rem(me + 1, devices), lax.rem(me + devices - 1, devices)
    cells = state.shape[1]

    loads = [
        pltpu.make_async_copy(state.at[0], fe.at[pl.ds(5, cells)], local_sem.at[0]),
        pltpu.make_async_copy(state.at[1], pe.at[pl.ds(4, cells)], local_sem.at[1]),
        pltpu.make_async_copy(fine, q, local_sem.at[2]),
    ]
    for load in loads:
        load.start()

    barrier = pltpu.get_barrier_semaphore()
    for neighbour in (left, right):
        pl.semaphore_signal(barrier, inc=1, device_id={"gx": neighbour}, device_id_type=MESH)
    pl.semaphore_wait(barrier, 2)

    def remote(src, dst, number, target):
        return pltpu.make_async_remote_copy(
            src_ref=src, dst_ref=dst, send_sem=send_sem.at[number], recv_sem=recv_sem.at[number],
            device_id={"gx": target}, device_id_type=MESH,
        )

    halo = [
        remote(state.at[0, pl.ds(cells - 5, 5)], fe.at[pl.ds(0, 5)], 0, right),
        remote(state.at[0, pl.ds(0, 5)], fe.at[pl.ds(cells + 5, 5)], 1, left),
        remote(state.at[1, pl.ds(cells - 4, 4)], pe.at[pl.ds(0, 4)], 2, right),
        remote(state.at[1, pl.ds(0, 4)], pe.at[pl.ds(cells + 4, 4)], 3, left),
    ]
    for copy in halo:
        copy.start()

    cz[...] = coarse_weights()
    inner, outer = fine_weights()
    fw[0:256] = inner
    fw[256:512] = outer
    wy, wzl, wzh, wx = boundary_weights()
    bw[0] = wy
    bw[1] = wzl
    bw[2] = wzh
    bw[3] = wx
    mw[...] = mean_weights()
    zeros8 = jnp.zeros((8, 1024), F32)
    for i in range(2):
        pad[i, 0:8] = zeros8
        pad[i, 40:48] = zeros8

    corner = []
    for dest in range(2):
        holder = me if dest == 0 else right
        for i in range(2):
            number = plan[holder * BOX_DEV + i]
            x, y, z = boxes[number, 0], boxes[number, 1], boxes[number, 2]
            corner.append((jnp.where(lax.div(x, jnp.int32(cells)) == me, 1, 0), y, z))

    def pick(index, values):
        out = values[-1]
        for number in range(len(values) - 2, -1, -1):
            out = jnp.where(index == number, values[number], out)
        return out

    def force(ref, base, start, n):
        at = start - base
        centre = ref[pl.ds(at, n)]
        near = ref[pl.ds(at - 1, n)] + ref[pl.ds(at + 1, n)]
        far = ref[pl.ds(at - 2, n)] + ref[pl.ds(at + 2, n)]
        near += roll(centre, 1, 1) + roll(centre, -1, 1)
        far += roll(centre, 2, 1) + roll(centre, -2, 1)
        hi, lo = halves(centre.reshape(n * 32, 256))
        along_z = (mm(hi, cz[...]) + mm(lo, cz[...])).reshape(n, 32, 256)
        lap = (16.0 * near - far + along_z - 90.0 * centre) * (1.0 / 12.0)
        return lap + centre * (centre * centre - 1.0)

    def fill_f2(start, n):
        f2[pl.ds(start + 4, n)] = fe[pl.ds(start + 5, n)] + 0.25 * pe[pl.ds(start + 4, n)]

    def stage1(start, n):
        slope = force(fe, -5, start, n)
        k1[pl.ds(start + 3, n)] = slope
        f3[pl.ds(start + 3, n)] = f2[pl.ds(start + 4, n)] + 0.0625 * slope

    def stage2(start, n):
        slope = force(f2, -4, start, n)
        k2[pl.ds(start + 2, n)] = slope
        f4[pl.ds(start + 2, n)] = fe[pl.ds(start + 5, n)] + 0.5 * pe[pl.ds(start + 4, n)] + 0.125 * slope

    def stage3(start, n):
        slope = force(f3, -3, start, n)
        one, two = k1[pl.ds(start + 3, n)], k2[pl.ds(start + 2, n)]
        nf[pl.ds(start + 1, n)] = (
            fe[pl.ds(start + 5, n)] + 0.5 * pe[pl.ds(start + 4, n)] + (1.0 / 24.0) * (one + two + slope)
        )
        k2[pl.ds(start + 2, n)] = one + 2.0 * two + 2.0 * slope

    def stage4(start, n):
        slope = force(f4, -2, start, n)
        npm[pl.ds(start, n)] = pe[pl.ds(start + 4, n)] + (1.0 / 12.0) * (k2[pl.ds(start + 2, n)] + slope)

    loads[0].wait()
    loads[1].wait()
    for s in range(0, 16, 4):
        fill_f2(s, 4)
    for s in range(2, 14, 4):
        stage1(s, 4)
        stage2(s, 4)
    loads[2].wait()
    for copy in halo:
        copy.wait()
    for s in (-4, 16):
        fill_f2(s, 4)
    for s in (-3, 14):
        stage1(s, 5)
    for s in (-2, 14):
        stage2(s, 4)
    for s in range(-1, 17, 6):
        stage3(s, 6)

    lane = iota((1, 128), 1)
    group = ((lane >> 6) << 1) + ((lane >> 4) & 1)
    lane_y = pick(group, [c[1] for c in corner])
    lane_z = pick(group, [c[2] for c in corner]) + (lane & 15)
    k = iota((256, 128), 0)
    hit = jnp.where(k == lane_z, 1.0, 0.0)
    raw = None
    rows8 = iota((8, 1), 0)
    row_box = rows8 >> 1
    row_y = pick(row_box, [c[1] for c in corner])
    row_z = pick(row_box, [c[2] for c in corner])
    row_z = jnp.where((rows8 & 1) == 0, row_z + 255, row_z + 16) & 255
    side_hit = jnp.where(iota((8, 256), 1) == row_z, 1.0, 0.0).astype(BF)
    for t, (ref, base) in enumerate(((fe, 4), (nf, 0))):
        body = ref[pl.ds(base + 1, cells)]
        rows = jnp.concatenate(
            [ref[base], ref[base + cells + 1], body[:, 31], body[:, 15], body[:, 16], body[:, 0]], axis=0
        )
        hi, lo = halves(rows)
        weight = jnp.where(((iota((256, 128), 1) >> 5) & 1) == t, hit, 0.0).astype(BF)
        part = mm(hi, weight) + mm(lo, weight)
        raw = part if raw is None else raw + part
        hi, lo = halves(body.reshape(cells * 32, 256))
        side = mm_nt(side_hit, hi) + mm_nt(side_hit, lo)
        sides[pl.ds(8 * t, 8)] = jnp.where(jnp.broadcast_to(row_y, (8, 512)) == 0, side, roll(side, -16, 1))
    low = jnp.broadcast_to(lane_y, (16, 128)) == 0
    faces[0:16] = jnp.where(low, raw[0:16], raw[16:32])
    faces[16:32] = jnp.where(low, raw[32:48], raw[48:64])
    faces[32:48] = jnp.where(low, raw[64:80], raw[80:96])
    faces[48:64] = jnp.where(low, raw[96:112], raw[112:128])
    patch = [remote(faces, faces_in, 4, right), remote(sides, sides_in, 5, right)]
    for copy in patch:
        copy.start()

    for s in range(0, 16, 4):
        stage4(s, 4)

    def inside(f):
        for i in range(2):
            pad[i, 8:40] = f[32 * i : 32 * i + 32]
        hi, lo = halves(f)
        none = jnp.zeros((64, 128), BF)

        def gathered(a):
            mid = jnp.concatenate([a[:, 256 * t : 256 * t + 256] for t in range(4)], axis=0)
            before = [none] + [a[:, 256 * t - 128 : 256 * t] for t in range(1, 4)]
            after = [a[:, 256 * t + 256 : 256 * t + 384] for t in range(3)] + [none]
            beside = jnp.concatenate(
                [jnp.concatenate(before, axis=0), jnp.concatenate(after, axis=0)], axis=1
            )
            return jnp.concatenate([mid, beside], axis=1)

        weights = fw[...]
        out = mm(gathered(hi), weights) + mm(gathered(lo), weights)
        along = jnp.concatenate([out[64 * t : 64 * t + 64] for t in range(4)], axis=1)

        def shifted(d):
            return jnp.concatenate([pad[i, 8 + d : 40 + d] for i in range(2)], axis=0)

        lap = 16.0 * (shifted(1) + shifted(-1)) - (shifted(2) + shifted(-2)) + along - 90.0 * f
        return lap * (1.0 / 3.0) + f * (f * f - 1.0)

    h = 0.25
    f = q[0].reshape(64, 1024)
    p = q[1].reshape(64, 1024)
    first = inside(f)
    second = inside(f + (h / 2) * p)

    for copy in patch:
        copy.wait()
    own = [c[0] for c in corner[:2]]
    lane_own = pick((lane >> 4) & 1, own)
    mixed = jnp.where(jnp.broadcast_to(lane_own, (64, 128)) == 1, faces[...], roll(faces_in[...], 64, 1))
    wide_lane = iota((128, 128), 1)
    same_group = ((wide_lane >> 4) & 3) == (iota((128, 128), 0) >> 5)
    y_faces = jnp.where(iota((16, 128), 1) < 64, mixed[32:48], roll(mixed[48:64], 64, 1))
    up = jnp.where(((iota((128, 16), 0) & 31) >> 1) == iota((128, 16), 1), 1.0, 0.0).astype(BF)
    hi, lo = halves(y_faces)
    wide = mm(up, hi) + mm(up, lo)
    wide = jnp.where(same_group, wide, 0.0)
    hi, lo = halves(wide)
    bound = mm(hi, bw[0]) + mm(lo, bw[0])
    stripe = (iota((8, 128), 1) >> 5) == (iota((8, 128), 0) >> 1)
    for side in range(2):
        blocks = []
        for t in range(2):
            for i in range(2):
                at = 8 * t + 2 * i + side
                line = jnp.where(own[i] == 1, sides[pl.ds(at, 1)], sides_in[pl.ds(at + 4, 1)])
                for tile in range(4):
                    piece = line[:, 128 * tile : 128 * tile + 128]
                    blocks.append(jnp.where(stripe, jnp.broadcast_to(piece, (8, 128)), 0.0))
        hi, lo = halves(jnp.concatenate(blocks, axis=0))
        bound += mm(hi, bw[1 + side]) + mm(lo, bw[1 + side])
    x_faces = jnp.concatenate([mixed[0:32]] * 4, axis=0)
    x_faces = jnp.where(same_group & (wide_lane < 64), x_faces, 0.0)
    hi, lo = halves(x_faces)
    spread = mm(hi, bw[3]) + mm(lo, bw[3])
    fits = (iota((128, 1024), 0) & 15) == (iota((128, 1024), 1) >> 6)
    spread = jnp.where(fits, spread, 0.0)
    kk, rr = iota((128, 128), 1), iota((128, 128), 0)
    lift = jnp.where((kk >> 5) == (rr >> 5), edge((kk >> 4) & 1, rr & 31), 0.0).astype(BF)
    hi, lo = halves(spread)
    bound += mm(lift, hi) + mm(lift, lo)
    bound = bound * (1.0 / 3.0)
    b_old = bound[0:64]
    b_diff = bound[64:128] - b_old

    for step in range(2):
        r = 0.5 * step
        if step == 1:
            first = inside(f)
            second = inside(f + (h / 2) * p)
        one = first + (b_old + r * b_diff)
        mid = b_old + (r + 0.25) * b_diff
        two = second + mid
        three = inside(f + (h / 2) * p + (h * h / 4) * one) + mid
        four = inside(f + h * p + (h * h / 2) * two) + (b_old + (r + 0.5) * b_diff)
        f = f + h * p + (h * h / 6) * (one + two + three)
        p = p + (h / 6) * (one + 2.0 * two + 2.0 * three + four)
    q[0] = f.reshape(2, 32, 1024)
    q[1] = p.reshape(2, 32, 1024)
    store_fine = pltpu.make_async_copy(q, fine_out, local_sem.at[2])
    store_fine.start()

    hi, lo = halves(jnp.concatenate([f, p], axis=0))
    flat = mm(hi, mw[...]) + mm(lo, mw[...])
    pair = jnp.where((iota((64, 128), 1) >> 1) == iota((64, 128), 0), 0.125, 0.0).astype(BF)
    hi, lo = halves(flat)
    means[...] = mm(pair, hi) + mm(pair, lo)
    back = remote(means, means_in, 6, left)
    back.start()

    eye = (iota((8, 128), 1) >> 4) == iota((8, 128), 0)
    z_lane = iota((16, 16, 256), 2)

    def insert(ref, i, keep, y, z):
        blocks = []
        for c in range(2):
            values = ref[pl.ds(32 * c + 16 * i, 16)]
            for x in range(16):
                for tile in range(2):
                    piece = values[x : x + 1, 128 * tile : 128 * tile + 128]
                    blocks.append(jnp.where(eye, jnp.broadcast_to(piece, (8, 128)), 0.0))
        hi, lo = halves(jnp.concatenate(blocks, axis=0))
        place = jnp.where((iota((128, 256), 0) & 15) + z == iota((128, 256), 1), 1.0, 0.0).astype(BF)
        block = (mm(hi, place) + mm(lo, place)).reshape(2, 16, 16, 256)
        for half in range(2):
            chosen = jnp.where(y == 16 * half, keep, 0)
            here = jnp.where((z_lane >> 4) == (z >> 4), chosen, 0) == 1
            rows = pl.ds(16 * half, 16)
            nf[pl.ds(1, cells), rows] = jnp.where(here, block[0], nf[pl.ds(1, cells), rows])
            npm[:, rows] = jnp.where(here, block[1], npm[:, rows])

    for i in range(2):
        insert(means, i, *corner[i])
    back.wait()
    for i in range(2):
        insert(means_in, i, *corner[2 + i])
    stores = [
        pltpu.make_async_copy(nf.at[pl.ds(1, cells)], coarse_out.at[0], local_sem.at[0]),
        pltpu.make_async_copy(npm, coarse_out.at[1], local_sem.at[1]),
    ]
    for store in stores:
        store.start()
    store_fine.wait()
    for store in stores:
        store.wait()


def shards(devices, state, fine_state, box_list, plan):
    cells, ny, nz = state.shape[1:]

    def slab(layers):
        return pltpu.VMEM((layers, ny, nz), F32)

    any_spec = pl.BlockSpec(memory_space=pl.ANY)
    smem_spec = pl.BlockSpec(memory_space=pltpu.SMEM)

    def body(*refs):
        kernel(devices, *refs)

    return pl.pallas_call(
        body,
        out_shape=(
            jax.ShapeDtypeStruct(state.shape, F32),
            jax.ShapeDtypeStruct(fine_state.shape, F32),
        ),
        in_specs=[any_spec, any_spec, smem_spec, smem_spec],
        out_specs=(any_spec, any_spec),
        scratch_shapes=[
            slab(cells + 10), slab(cells + 8),
            slab(cells + 8), slab(cells + 6), slab(cells + 4),
            slab(cells + 6), slab(cells + 4), slab(cells + 2), slab(cells),
            pltpu.VMEM(fine_state.shape, F32),
            pltpu.VMEM((2, 48, 1024), F32),
            pltpu.VMEM((64, 128), F32), pltpu.VMEM((64, 128), F32),
            pltpu.VMEM((16, 512), F32), pltpu.VMEM((16, 512), F32),
            pltpu.VMEM((64, 256), F32), pltpu.VMEM((64, 256), F32),
            pltpu.VMEM((256, 256), BF), pltpu.VMEM((512, 256), BF),
            pltpu.VMEM((4, 128, 1024), BF), pltpu.VMEM((1024, 256), BF),
            pltpu.SemaphoreType.DMA((3,)),
            pltpu.SemaphoreType.DMA((7,)),
            pltpu.SemaphoreType.DMA((7,)),
        ],
        compiler_params=pltpu.CompilerParams(
            collective_id=0, has_side_effects=True, vmem_limit_bytes=48 * 1024 * 1024
        ),
        cost_estimate=pl.CostEstimate(flops=10**9, bytes_accessed=3 * 2**20, transcendentals=0),
        name="refined_step",
    )(state, fine_state, box_list, plan)


def solution(mesh):
    devices = mesh.shape["gx"]

    def local(*args):
        return shards(devices, *args)

    return jax.shard_map(
        local,
        mesh=mesh,
        in_specs=(
            P(None, ("ens", "gx"), None, None),
            P(None, ("ens", "gx"), None, None),
            P("ens", None),
            P("ens"),
        ),
        out_specs=(P(None, ("ens", "gx"), None, None), P(None, ("ens", "gx"), None, None)),
        check_vma=False,
    )
```

```python
import jax
import jax.numpy as jnp
from jax import lax
from jax.experimental import pallas as pl
from jax.experimental.pallas import tpu as pltpu
from jax.sharding import PartitionSpec as P

FB = 32
BOX_DEV = 2
MESH = pl.DeviceIdType.MESH
BF = jnp.bfloat16
F32 = jnp.float32


def iota(shape, dim):
    return lax.broadcasted_iota(jnp.int32, shape, dim)


def halves(a):
    hi = a.astype(BF)
    lo = (a - hi.astype(F32)).astype(BF)
    return hi, lo


def mm(a, b):
    return jnp.dot(a, b, preferred_element_type=F32)


def mm_nt(a, b):
    return lax.dot_general(a, b, (((1,), (1,)), ((), ())), preferred_element_type=F32)


def star(d):
    d = jnp.abs(d)
    return jnp.where(d == 1, 16.0, jnp.where(d == 2, -1.0, 0.0))


def edge(side, j):
    d = jnp.where(side == 0, j, 31 - j)
    return jnp.where(d == 0, 15.0, jnp.where(d == 1, -1.0, 0.0))


def coarse_weights():
    k, j = iota((256, 256), 0), iota((256, 256), 1)
    d = (j - k) & 255
    d = jnp.minimum(d, 256 - d)
    return star(d).astype(BF)


def fine_weights():
    k, j = iota((256, 256), 0), iota((256, 256), 1)
    jy, jz = j >> 5, j & 31
    ky, kz = k >> 5, k & 31
    inner = jnp.where(ky == jy, star(kz - jz), 0.0) + jnp.where(kz == jz, star(ky - jy), 0.0)
    far = jnp.where(k < 128, ky - 4, ky + 4)
    outer = jnp.where(kz == jz, star(far - jy), 0.0)
    return inner.astype(BF), outer.astype(BF)


def boundary_weights():
    k, j = iota((128, 1024), 0), iota((128, 1024), 1)
    y, z = j >> 5, j & 31
    wy = jnp.where((k & 15) == (z >> 1), edge(k >> 6, y), 0.0).astype(BF)
    wzl = jnp.where((k & 31) == (y >> 1), edge(0, z), 0.0).astype(BF)
    wzh = jnp.where((k & 31) == (y >> 1), edge(1, z), 0.0).astype(BF)
    wx = jnp.where((k & 15) == (z >> 1), 1.0, 0.0).astype(BF)
    return wy, wzl, wzh, wx


def mean_weights():
    k, j = iota((1024, 256), 0), iota((1024, 256), 1)
    return jnp.where(((k >> 6) == (j >> 4)) & (((k & 31) >> 1) == (j & 15)), 1.0, 0.0).astype(BF)


def roll(a, shift, axis):
    return pltpu.roll(a, shift % a.shape[axis], axis)


def kernel(
    devices,
    state, fine, boxes_hbm, plan_hbm,
    coarse_out, fine_out,
    fe, pe, f2, f3, f4, k1, k2, nf, npm,
    q, pad, patches, patches_in, means, means_in, cz, fw, bw, mw, boxes, plan,
    local_sem, send_sem, recv_sem,
):
    me = lax.axis_index("gx")
    right, left = lax.rem(me + 1, devices), lax.rem(me + devices - 1, devices)
    cells = state.shape[1]

    barrier = pltpu.get_barrier_semaphore()
    for neighbour in (left, right):
        pl.semaphore_signal(barrier, inc=1, device_id={"gx": neighbour}, device_id_type=MESH)
    loads = [
        pltpu.make_async_copy(state.at[0], fe.at[pl.ds(5, cells)], local_sem.at[0]),
        pltpu.make_async_copy(state.at[1], pe.at[pl.ds(4, cells)], local_sem.at[1]),
        pltpu.make_async_copy(fine, q, local_sem.at[2]),
        pltpu.make_async_copy(boxes_hbm, boxes, local_sem.at[3]),
        pltpu.make_async_copy(plan_hbm, plan, local_sem.at[4]),
    ]
    for load in loads:
        load.start()

    pl.semaphore_wait(barrier, 2)

    def remote(src, dst, number, target):
        return pltpu.make_async_remote_copy(
            src_ref=src, dst_ref=dst, send_sem=send_sem.at[number], recv_sem=recv_sem.at[number],
            device_id={"gx": target}, device_id_type=MESH,
        )

    halo = [
        remote(state.at[0, pl.ds(cells - 5, 5)], fe.at[pl.ds(0, 5)], 0, right),
        remote(state.at[0, pl.ds(0, 5)], fe.at[pl.ds(cells + 5, 5)], 1, left),
        remote(state.at[1, pl.ds(cells - 4, 4)], pe.at[pl.ds(0, 4)], 2, right),
        remote(state.at[1, pl.ds(0, 4)], pe.at[pl.ds(cells + 4, 4)], 3, left),
    ]
    for copy in halo:
        copy.start()

    cz[...] = coarse_weights()
    inner, outer = fine_weights()
    fw[0:256] = inner
    fw[256:512] = outer
    wy, wzl, wzh, wx = boundary_weights()
    bw[0] = wy
    bw[1] = wzl
    bw[2] = wzh
    bw[3] = wx
    mw[...] = mean_weights()
    zeros8 = jnp.zeros((8, 1024), F32)
    for i in range(2):
        pad[i, 0:8] = zeros8
        pad[i, 40:48] = zeros8

    loads[3].wait()
    loads[4].wait()
    corner = []
    for dest in range(2):
        holder = me if dest == 0 else right
        for i in range(2):
            number = plan[holder * BOX_DEV + i]
            x, y, z = boxes[0, number], boxes[1, number], boxes[2, number]
            corner.append((jnp.where(lax.div(x, jnp.int32(cells)) == me, 1, 0), y, z))

    def pick(index, values):
        out = values[-1]
        for number in range(len(values) - 2, -1, -1):
            out = jnp.where(index == number, values[number], out)
        return out

    def force(ref, base, start, n):
        at = start - base
        centre = ref[pl.ds(at, n)]
        near = ref[pl.ds(at - 1, n)] + ref[pl.ds(at + 1, n)]
        far = ref[pl.ds(at - 2, n)] + ref[pl.ds(at + 2, n)]
        near += roll(centre, 1, 1) + roll(centre, -1, 1)
        far += roll(centre, 2, 1) + roll(centre, -2, 1)
        hi, lo = halves(centre.reshape(n * 32, 256))
        along_z = (mm(hi, cz[...]) + mm(lo, cz[...])).reshape(n, 32, 256)
        lap = (16.0 * near - far + along_z - 90.0 * centre) * (1.0 / 12.0)
        return lap + centre * (centre * centre - 1.0)

    def fill_f2(start, n):
        f2[pl.ds(start + 4, n)] = fe[pl.ds(start + 5, n)] + 0.25 * pe[pl.ds(start + 4, n)]

    def stage1(start, n):
        slope = force(fe, -5, start, n)
        k1[pl.ds(start + 3, n)] = slope
        f3[pl.ds(start + 3, n)] = f2[pl.ds(start + 4, n)] + 0.0625 * slope

    def stage2(start, n):
        slope = force(f2, -4, start, n)
        k2[pl.ds(start + 2, n)] = slope
        f4[pl.ds(start + 2, n)] = fe[pl.ds(start + 5, n)] + 0.5 * pe[pl.ds(start + 4, n)] + 0.125 * slope

    def stage3(start, n):
        slope = force(f3, -3, start, n)
        one, two = k1[pl.ds(start + 3, n)], k2[pl.ds(start + 2, n)]
        nf[pl.ds(start + 1, n)] = (
            fe[pl.ds(start + 5, n)] + 0.5 * pe[pl.ds(start + 4, n)] + (1.0 / 24.0) * (one + two + slope)
        )
        k2[pl.ds(start + 2, n)] = one + 2.0 * two + 2.0 * slope

    def stage4(start, n):
        slope = force(f4, -2, start, n)
        npm[pl.ds(start, n)] = pe[pl.ds(start + 4, n)] + (1.0 / 12.0) * (k2[pl.ds(start + 2, n)] + slope)

    loads[0].wait()
    loads[1].wait()
    for s in range(0, 16, 4):
        fill_f2(s, 4)
    for s in range(2, 14, 4):
        stage1(s, 4)
        stage2(s, 4)
    stage3(4, 4)
    stage3(8, 4)
    loads[2].wait()

    def inside(f):
        for i in range(2):
            pad[i, 8:40] = f[32 * i : 32 * i + 32]
        hi, lo = halves(f)
        none = jnp.zeros((64, 128), BF)

        def gathered(a):
            mid = jnp.concatenate([a[:, 256 * t : 256 * t + 256] for t in range(4)], axis=0)
            before = [none] + [a[:, 256 * t - 128 : 256 * t] for t in range(1, 4)]
            after = [a[:, 256 * t + 256 : 256 * t + 384] for t in range(3)] + [none]
            beside = jnp.concatenate(
                [jnp.concatenate(before, axis=0), jnp.concatenate(after, axis=0)], axis=1
            )
            return jnp.concatenate([mid, beside], axis=1)

        weights = fw[...]
        out = mm(gathered(hi), weights) + mm(gathered(lo), weights)
        along = jnp.concatenate([out[64 * t : 64 * t + 64] for t in range(4)], axis=1)

        def shifted(d):
            return jnp.concatenate([pad[i, 8 + d : 40 + d] for i in range(2)], axis=0)

        lap = 16.0 * (shifted(1) + shifted(-1)) - (shifted(2) + shifted(-2)) + along - 90.0 * f
        return lap * (1.0 / 3.0) + f * (f * f - 1.0)

    h = 0.25
    f = q[0].reshape(64, 1024)
    p = q[1].reshape(64, 1024)
    first = inside(f)
    second = inside(f + (h / 2) * p)

    for copy in halo:
        copy.wait()
    for s in (-4, 16):
        fill_f2(s, 4)
    for s in (-3, 14):
        stage1(s, 5)
    for s in (-2, 14):
        stage2(s, 4)
    for s in (-1, 12):
        stage3(s, 5)

    lane = iota((1, 128), 1)
    group = ((lane >> 6) << 1) + ((lane >> 4) & 1)
    lane_y = pick(group, [c[1] for c in corner])
    lane_z = pick(group, [c[2] for c in corner]) + (lane & 15)
    k = iota((256, 128), 0)
    hit = jnp.where(k == lane_z, 1.0, 0.0)
    raw = None
    rows8 = iota((8, 1), 0)
    row_box = rows8 >> 1
    row_y = pick(row_box, [c[1] for c in corner])
    row_z = pick(row_box, [c[2] for c in corner])
    row_z = jnp.where((rows8 & 1) == 0, row_z + 255, row_z + 16) & 255
    side_hit = jnp.where(iota((8, 256), 1) == row_z, 1.0, 0.0).astype(BF)
    for t, (ref, base) in enumerate(((fe, 4), (nf, 0))):
        body = ref[pl.ds(base + 1, cells)]
        rows = jnp.concatenate(
            [ref[base], ref[base + cells + 1], body[:, 31], body[:, 15], body[:, 16], body[:, 0]], axis=0
        )
        hi, lo = halves(rows)
        weight = jnp.where(((iota((256, 128), 1) >> 5) & 1) == t, hit, 0.0).astype(BF)
        part = mm(hi, weight) + mm(lo, weight)
        raw = part if raw is None else raw + part
        hi, lo = halves(body.reshape(cells * 32, 256))
        side = mm_nt(side_hit, hi) + mm_nt(side_hit, lo)
        side = jnp.where(jnp.broadcast_to(row_y, (8, 512)) == 0, side, roll(side, -16, 1))
        for dest in range(2):
            for tile in range(4):
                patches[dest, pl.ds(32 + 8 * tile + 4 * t, 4)] = side[
                    4 * dest : 4 * dest + 4, 128 * tile : 128 * tile + 128
                ]
    low = jnp.broadcast_to(lane_y, (16, 128)) == 0
    x_part = jnp.concatenate(
        [jnp.where(low, raw[0:16], raw[16:32]), jnp.where(low, raw[32:48], raw[48:64])], axis=0
    )
    y_part = jnp.concatenate(
        [jnp.where(low, raw[64:80], raw[80:96]), jnp.where(low, raw[96:112], raw[112:128])], axis=0
    )
    first_half = iota((32, 128), 1) < 64
    patches[0, 0:32] = jnp.where(first_half, x_part, roll(y_part, 64, 1))
    patches[1, 0:32] = jnp.where(first_half, roll(x_part, 64, 1), y_part)
    patch = [remote(patches.at[1], patches_in, 4, right)]
    for copy in patch:
        copy.start()

    for s in range(0, 16, 4):
        stage4(s, 4)

    for copy in patch:
        copy.wait()
    own = [c[0] for c in corner[:2]]
    lane_own = pick((lane >> 4) & 1, own)
    mixed = jnp.where(jnp.broadcast_to(lane_own, (32, 128)) == 1, patches[0, 0:32], patches_in[0:32])
    wide_lane = iota((128, 128), 1)
    same_group = ((wide_lane >> 4) & 3) == (iota((128, 128), 0) >> 5)
    y_faces = jnp.where(iota((16, 128), 1) < 64, roll(mixed[0:16], 64, 1), mixed[16:32])
    up = jnp.where(((iota((128, 16), 0) & 31) >> 1) == iota((128, 16), 1), 1.0, 0.0).astype(BF)
    hi, lo = halves(y_faces)
    wide = mm(up, hi) + mm(up, lo)
    wide = jnp.where(same_group, wide, 0.0)
    hi, lo = halves(wide)
    bound = mm(hi, bw[0]) + mm(lo, bw[0])
    stripe = (iota((8, 128), 1) >> 5) == (iota((8, 128), 0) >> 1)
    for side in range(2):
        blocks = []
        for t in range(2):
            for i in range(2):
                for tile in range(4):
                    at = pl.ds(32 + 8 * tile + 4 * t + 2 * i + side, 1)
                    piece = jnp.where(own[i] == 1, patches[0, at], patches_in[at])
                    blocks.append(jnp.where(stripe, jnp.broadcast_to(piece, (8, 128)), 0.0))
        hi, lo = halves(jnp.concatenate(blocks, axis=0))
        bound += mm(hi, bw[1 + side]) + mm(lo, bw[1 + side])
    x_faces = jnp.concatenate([mixed] * 4, axis=0)
    x_faces = jnp.where(same_group & (wide_lane < 64), x_faces, 0.0)
    hi, lo = halves(x_faces)
    spread = mm(hi, bw[3]) + mm(lo, bw[3])
    fits = (iota((128, 1024), 0) & 15) == (iota((128, 1024), 1) >> 6)
    spread = jnp.where(fits, spread, 0.0)
    kk, rr = iota((128, 128), 1), iota((128, 128), 0)
    lift = jnp.where((kk >> 5) == (rr >> 5), edge((kk >> 4) & 1, rr & 31), 0.0).astype(BF)
    hi, lo = halves(spread)
    bound += mm(lift, hi) + mm(lift, lo)
    bound = bound * (1.0 / 3.0)
    b_old = bound[0:64]
    b_diff = bound[64:128] - b_old

    pair = jnp.where((iota((32, 64), 1) >> 1) == iota((32, 64), 0), 0.125, 0.0).astype(BF)
    sent = []

    def finish(c, values):
        q[c] = values.reshape(2, 32, 1024)
        hi, lo = halves(values)
        flat = mm(hi, mw[...]) + mm(lo, mw[...])
        hi, lo = halves(flat)
        means[c] = mm(pair, hi) + mm(pair, lo)
        back = remote(means.at[c], means_in.at[c], 5 + c, left)
        back.start()
        store = pltpu.make_async_copy(q.at[c], fine_out.at[c], local_sem.at[2 + c])
        store.start()
        sent.append((back, store))

    for step in range(2):
        r = 0.5 * step
        if step == 1:
            first = inside(f)
            second = inside(f + (h / 2) * p)
        one = first + (b_old + r * b_diff)
        mid = b_old + (r + 0.25) * b_diff
        two = second + mid
        three = inside(f + (h / 2) * p + (h * h / 4) * one) + mid
        new = f + h * p + (h * h / 6) * (one + two + three)
        if step == 1:
            finish(0, new)
        four = inside(f + h * p + (h * h / 2) * two) + (b_old + (r + 0.5) * b_diff)
        f = new
        p = p + (h / 6) * (one + 2.0 * two + 2.0 * three + four)
    finish(1, p)

    eye = (iota((8, 128), 1) >> 4) == iota((8, 128), 0)
    z_lane = iota((16, 16, 256), 2)

    into = (nf.at[pl.ds(1, cells)], npm)

    def insert(ref, c, i, keep, y, z):
        values = ref[c, pl.ds(16 * i, 16)]
        blocks = []
        for x in range(16):
            for tile in range(2):
                piece = values[x : x + 1, 128 * tile : 128 * tile + 128]
                blocks.append(jnp.where(eye, jnp.broadcast_to(piece, (8, 128)), 0.0))
        hi, lo = halves(jnp.concatenate(blocks, axis=0))
        place = jnp.where((iota((128, 256), 0) & 15) + z == iota((128, 256), 1), 1.0, 0.0).astype(BF)
        block = (mm(hi, place) + mm(lo, place)).reshape(16, 16, 256)
        for half in range(2):
            chosen = jnp.where(y == 16 * half, keep, 0)
            here = jnp.where((z_lane >> 4) == (z >> 4), chosen, 0) == 1
            rows = pl.ds(16 * half, 16)
            into[c][:, rows] = jnp.where(here, block, into[c][:, rows])

    stores = []
    for c in range(2):
        for i in range(2):
            insert(means, c, i, *corner[i])
    for c in range(2):
        sent[c][0].wait()
        for i in range(2):
            insert(means_in, c, i, *corner[2 + i])
        store = pltpu.make_async_copy(into[c], coarse_out.at[c], local_sem.at[c])
        store.start()
        stores.append(store)
    for c in range(2):
        sent[c][1].wait()
        stores[c].wait()


def shards(devices, state, fine_state, box_list, plan):
    boxes = box_list.T
    cells, ny, nz = state.shape[1:]

    def slab(layers):
        return pltpu.VMEM((layers, ny, nz), F32)

    any_spec = pl.BlockSpec(memory_space=pl.ANY)
    hbm_spec = pl.BlockSpec(memory_space=pltpu.HBM)

    def body(*refs):
        kernel(devices, *refs)

    return pl.pallas_call(
        body,
        out_shape=(
            jax.ShapeDtypeStruct(state.shape, F32),
            jax.ShapeDtypeStruct(fine_state.shape, F32),
        ),
        in_specs=[hbm_spec, hbm_spec, hbm_spec, hbm_spec],
        out_specs=(any_spec, any_spec),
        scratch_shapes=[
            slab(cells + 10), slab(cells + 8),
            slab(cells + 8), slab(cells + 6), slab(cells + 4),
            slab(cells + 6), slab(cells + 4), slab(cells + 2), slab(cells),
            pltpu.VMEM(fine_state.shape, F32),
            pltpu.VMEM((2, 48, 1024), F32),
            pltpu.VMEM((2, 64, 128), F32), pltpu.VMEM((64, 128), F32),
            pltpu.VMEM((2, 32, 256), F32), pltpu.VMEM((2, 32, 256), F32),
            pltpu.VMEM((256, 256), BF), pltpu.VMEM((512, 256), BF),
            pltpu.VMEM((4, 128, 1024), BF), pltpu.VMEM((1024, 256), BF),
            pltpu.SMEM(boxes.shape, jnp.int32), pltpu.SMEM(plan.shape, jnp.int32),
            pltpu.SemaphoreType.DMA((5,)),
            pltpu.SemaphoreType.DMA((7,)),
            pltpu.SemaphoreType.DMA((7,)),
        ],
        compiler_params=pltpu.CompilerParams(
            collective_id=0, has_side_effects=True, vmem_limit_bytes=48 * 1024 * 1024
        ),
        cost_estimate=pl.CostEstimate(flops=10**9, bytes_accessed=3 * 2**20, transcendentals=0),
        name="refined_step",
    )(state, fine_state, boxes, plan)


def solution(mesh):
    devices = mesh.shape["gx"]

    def local(*args):
        return shards(devices, *args)

    return jax.shard_map(
        local,
        mesh=mesh,
        in_specs=(
            P(None, ("ens", "gx"), None, None),
            P(None, ("ens", "gx"), None, None),
            P("ens", None),
            P("ens"),
        ),
        out_specs=(P(None, ("ens", "gx"), None, None), P(None, ("ens", "gx"), None, None)),
        check_vma=False,
    )
```

```python
import jax
import jax.numpy as jnp
from jax import lax
from jax.experimental import pallas as pl
from jax.experimental.pallas import tpu as pltpu
from jax.sharding import PartitionSpec as P

FB = 32
BOX_DEV = 2
VMEM_LIMIT = 62 * 1024 * 1024
MESH = pl.DeviceIdType.MESH
BF = jnp.bfloat16
F32 = jnp.float32


def iota(shape, dim):
    return lax.broadcasted_iota(jnp.int32, shape, dim)


def halves(a):
    hi = a.astype(BF)
    lo = (a - hi.astype(F32)).astype(BF)
    return hi, lo


def mm(a, b):
    return jnp.dot(a, b, preferred_element_type=F32)


def mm_nt(a, b):
    return lax.dot_general(a, b, (((1,), (1,)), ((), ())), preferred_element_type=F32)


def star(d):
    d = jnp.abs(d)
    return jnp.where(d == 1, 16.0, jnp.where(d == 2, -1.0, 0.0))


def edge(side, j):
    d = jnp.where(side == 0, j, 31 - j)
    return jnp.where(d == 0, 15.0, jnp.where(d == 1, -1.0, 0.0))


def coarse_weights():
    k, j = iota((256, 256), 0), iota((256, 256), 1)
    d = (j - k) & 255
    d = jnp.minimum(d, 256 - d)
    return star(d).astype(BF)


def fine_weights():
    k, j = iota((256, 256), 0), iota((256, 256), 1)
    jy, jz = j >> 5, j & 31
    ky, kz = k >> 5, k & 31
    inner = jnp.where(ky == jy, star(kz - jz), 0.0) + jnp.where(kz == jz, star(ky - jy), 0.0)
    far = jnp.where(k < 128, ky - 4, ky + 4)
    outer = jnp.where(kz == jz, star(far - jy), 0.0)
    return inner.astype(BF), outer.astype(BF)


def boundary_weights():
    k, j = iota((128, 1024), 0), iota((128, 1024), 1)
    y, z = j >> 5, j & 31
    wy = jnp.where((k & 15) == (z >> 1), edge(k >> 6, y), 0.0).astype(BF)
    wzl = jnp.where((k & 31) == (y >> 1), edge(0, z), 0.0).astype(BF)
    wzh = jnp.where((k & 31) == (y >> 1), edge(1, z), 0.0).astype(BF)
    wx = jnp.where((k & 15) == (z >> 1), 1.0, 0.0).astype(BF)
    return wy, wzl, wzh, wx


def mean_weights():
    k, j = iota((1024, 256), 0), iota((1024, 256), 1)
    return jnp.where(((k >> 6) == (j >> 4)) & (((k & 31) >> 1) == (j & 15)), 1.0, 0.0).astype(BF)


def roll(a, shift, axis):
    return pltpu.roll(a, shift % a.shape[axis], axis)


def kernel(
    devices,
    state, fine, boxes_hbm, plan_hbm,
    coarse_out, fine_out,
    fe, pe, f2, f3, f4, k1, k2, nf,
    q, pad, patches, patches_in, means, means_in, cz, fw, bw, mw, boxes, plan,
    local_sem, send_sem, recv_sem,
):
    me = lax.axis_index("gx")
    right, left = lax.rem(me + 1, devices), lax.rem(me + devices - 1, devices)
    cells = state.shape[1]

    barrier = pltpu.get_barrier_semaphore()
    for neighbour in (left, right):
        pl.semaphore_signal(barrier, inc=1, device_id={"gx": neighbour}, device_id_type=MESH)
    loads = [
        pltpu.make_async_copy(state.at[0], fe.at[pl.ds(5, cells)], local_sem.at[0]),
        pltpu.make_async_copy(state.at[1], pe.at[pl.ds(4, cells)], local_sem.at[1]),
        pltpu.make_async_copy(fine, q, local_sem.at[2]),
        pltpu.make_async_copy(boxes_hbm, boxes, local_sem.at[3]),
        pltpu.make_async_copy(plan_hbm, plan, local_sem.at[4]),
    ]
    for load in loads:
        load.start()

    pl.semaphore_wait(barrier, 2)

    def remote(src, dst, number, target):
        return pltpu.make_async_remote_copy(
            src_ref=src, dst_ref=dst, send_sem=send_sem.at[number], recv_sem=recv_sem.at[number],
            device_id={"gx": target}, device_id_type=MESH,
        )

    halo = [
        remote(state.at[0, pl.ds(cells - 5, 5)], fe.at[pl.ds(0, 5)], 0, right),
        remote(state.at[0, pl.ds(0, 5)], fe.at[pl.ds(cells + 5, 5)], 1, left),
        remote(state.at[1, pl.ds(cells - 4, 4)], pe.at[pl.ds(0, 4)], 2, right),
        remote(state.at[1, pl.ds(0, 4)], pe.at[pl.ds(cells + 4, 4)], 3, left),
    ]
    for copy in halo:
        copy.start()

    cz[...] = coarse_weights()
    inner, outer = fine_weights()
    fw[0:256] = inner
    fw[256:512] = outer
    wy, wzl, wzh, wx = boundary_weights()
    bw[0] = wy
    bw[1] = wzl
    bw[2] = wzh
    bw[3] = wx
    mw[...] = mean_weights()
    zeros8 = jnp.zeros((8, 1024), F32)
    for i in range(2):
        pad[i, 0:8] = zeros8
        pad[i, 40:48] = zeros8

    loads[3].wait()
    loads[4].wait()
    corner = []
    for dest in range(2):
        holder = me if dest == 0 else right
        for i in range(2):
            number = plan[holder * BOX_DEV + i]
            x, y, z = boxes[0, number], boxes[1, number], boxes[2, number]
            corner.append((jnp.where(lax.div(x, jnp.int32(cells)) == me, 1, 0), y, z))

    def pick(index, values):
        out = values[-1]
        for number in range(len(values) - 2, -1, -1):
            out = jnp.where(index == number, values[number], out)
        return out

    def force(ref, base, start, n):
        at = start - base
        centre = ref[pl.ds(at, n)]
        near = ref[pl.ds(at - 1, n)] + ref[pl.ds(at + 1, n)]
        far = ref[pl.ds(at - 2, n)] + ref[pl.ds(at + 2, n)]
        near += roll(centre, 1, 1) + roll(centre, -1, 1)
        far += roll(centre, 2, 1) + roll(centre, -2, 1)
        hi, lo = halves(centre.reshape(n * 32, 256))
        along_z = (mm(hi, cz[...]) + mm(lo, cz[...])).reshape(n, 32, 256)
        lap = (16.0 * near - far + along_z - 90.0 * centre) * (1.0 / 12.0)
        return lap + centre * (centre * centre - 1.0)

    def fill_f2(start, n):
        f2[pl.ds(start + 4, n)] = fe[pl.ds(start + 5, n)] + 0.25 * pe[pl.ds(start + 4, n)]

    def stage1(start, n):
        slope = force(fe, -5, start, n)
        k1[pl.ds(start + 3, n)] = slope
        f3[pl.ds(start + 3, n)] = f2[pl.ds(start + 4, n)] + 0.0625 * slope

    def stage2(start, n):
        slope = force(f2, -4, start, n)
        k2[pl.ds(start + 2, n)] = slope
        f4[pl.ds(start + 2, n)] = fe[pl.ds(start + 5, n)] + 0.5 * pe[pl.ds(start + 4, n)] + 0.125 * slope

    def stage3(start, n):
        slope = force(f3, -3, start, n)
        one, two = k1[pl.ds(start + 3, n)], k2[pl.ds(start + 2, n)]
        nf[pl.ds(start + 1, n)] = (
            fe[pl.ds(start + 5, n)] + 0.5 * pe[pl.ds(start + 4, n)] + (1.0 / 24.0) * (one + two + slope)
        )
        k2[pl.ds(start + 2, n)] = one + 2.0 * two + 2.0 * slope

    def stage4(start, n):
        slope = force(f4, -2, start, n)
        coarse_out[1, pl.ds(start, n)] = pe[pl.ds(start + 4, n)] + (1.0 / 12.0) * (k2[pl.ds(start + 2, n)] + slope)

    loads[0].wait()
    loads[1].wait()
    for s in range(0, 16, 4):
        fill_f2(s, 4)
    for s in range(2, 14, 4):
        stage1(s, 4)
        stage2(s, 4)
    stage3(4, 4)
    stage3(8, 4)
    loads[2].wait()

    def inside(f):
        for i in range(2):
            pad[i, 8:40] = f[32 * i : 32 * i + 32]
        hi, lo = halves(f)
        none = jnp.zeros((64, 128), BF)

        def gathered(a):
            mid = jnp.concatenate([a[:, 256 * t : 256 * t + 256] for t in range(4)], axis=0)
            before = [none] + [a[:, 256 * t - 128 : 256 * t] for t in range(1, 4)]
            after = [a[:, 256 * t + 256 : 256 * t + 384] for t in range(3)] + [none]
            beside = jnp.concatenate(
                [jnp.concatenate(before, axis=0), jnp.concatenate(after, axis=0)], axis=1
            )
            return jnp.concatenate([mid, beside], axis=1)

        weights = fw[...]
        out = mm(gathered(hi), weights) + mm(gathered(lo), weights)
        along = jnp.concatenate([out[64 * t : 64 * t + 64] for t in range(4)], axis=1)

        def shifted(d):
            return jnp.concatenate([pad[i, 8 + d : 40 + d] for i in range(2)], axis=0)

        lap = 16.0 * (shifted(1) + shifted(-1)) - (shifted(2) + shifted(-2)) + along - 90.0 * f
        return lap * (1.0 / 3.0) + f * (f * f - 1.0)

    h = 0.25
    f = q[0].reshape(64, 1024)
    p = q[1].reshape(64, 1024)
    first = inside(f)
    second = inside(f + (h / 2) * p)

    for copy in halo:
        copy.wait()
    for s in (-4, 16):
        fill_f2(s, 4)
    for s in (-3, 14):
        stage1(s, 5)
    for s in (-2, 14):
        stage2(s, 4)
    for s in (-1, 12):
        stage3(s, 5)

    lane = iota((1, 128), 1)
    group = ((lane >> 6) << 1) + ((lane >> 4) & 1)
    lane_y = pick(group, [c[1] for c in corner])
    lane_z = pick(group, [c[2] for c in corner]) + (lane & 15)
    k = iota((256, 128), 0)
    hit = jnp.where(k == lane_z, 1.0, 0.0)
    raw = None
    rows8 = iota((8, 1), 0)
    row_box = rows8 >> 1
    row_y = pick(row_box, [c[1] for c in corner])
    row_z = pick(row_box, [c[2] for c in corner])
    row_z = jnp.where((rows8 & 1) == 0, row_z + 255, row_z + 16) & 255
    side_hit = jnp.where(iota((8, 256), 1) == row_z, 1.0, 0.0).astype(BF)
    for t, (ref, base) in enumerate(((fe, 4), (nf, 0))):
        body = ref[pl.ds(base + 1, cells)]
        rows = jnp.concatenate(
            [ref[base], ref[base + cells + 1], body[:, 31], body[:, 15], body[:, 16], body[:, 0]], axis=0
        )
        hi, lo = halves(rows)
        weight = jnp.where(((iota((256, 128), 1) >> 5) & 1) == t, hit, 0.0).astype(BF)
        part = mm(hi, weight) + mm(lo, weight)
        raw = part if raw is None else raw + part
        hi, lo = halves(body.reshape(cells * 32, 256))
        side = mm_nt(side_hit, hi) + mm_nt(side_hit, lo)
        side = jnp.where(jnp.broadcast_to(row_y, (8, 512)) == 0, side, roll(side, -16, 1))
        for dest in range(2):
            for tile in range(4):
                patches[dest, pl.ds(32 + 8 * tile + 4 * t, 4)] = side[
                    4 * dest : 4 * dest + 4, 128 * tile : 128 * tile + 128
                ]
    low = jnp.broadcast_to(lane_y, (16, 128)) == 0
    x_part = jnp.concatenate(
        [jnp.where(low, raw[0:16], raw[16:32]), jnp.where(low, raw[32:48], raw[48:64])], axis=0
    )
    y_part = jnp.concatenate(
        [jnp.where(low, raw[64:80], raw[80:96]), jnp.where(low, raw[96:112], raw[112:128])], axis=0
    )
    first_half = iota((32, 128), 1) < 64
    patches[0, 0:32] = jnp.where(first_half, x_part, roll(y_part, 64, 1))
    patches[1, 0:32] = jnp.where(first_half, roll(x_part, 64, 1), y_part)
    patch = [remote(patches.at[1], patches_in, 4, right)]
    for copy in patch:
        copy.start()

    new_field = pltpu.make_async_copy(nf.at[pl.ds(1, cells)], coarse_out.at[0], local_sem.at[0])
    new_field.start()
    for s in range(0, 16, 4):
        stage4(s, 4)

    for copy in patch:
        copy.wait()
    own = [c[0] for c in corner[:2]]
    lane_own = pick((lane >> 4) & 1, own)
    mixed = jnp.where(jnp.broadcast_to(lane_own, (32, 128)) == 1, patches[0, 0:32], patches_in[0:32])
    wide_lane = iota((128, 128), 1)
    same_group = ((wide_lane >> 4) & 3) == (iota((128, 128), 0) >> 5)
    y_faces = jnp.where(iota((16, 128), 1) < 64, roll(mixed[0:16], 64, 1), mixed[16:32])
    up = jnp.where(((iota((128, 16), 0) & 31) >> 1) == iota((128, 16), 1), 1.0, 0.0).astype(BF)
    hi, lo = halves(y_faces)
    wide = mm(up, hi) + mm(up, lo)
    wide = jnp.where(same_group, wide, 0.0)
    hi, lo = halves(wide)
    bound = mm(hi, bw[0]) + mm(lo, bw[0])
    stripe = (iota((8, 128), 1) >> 5) == (iota((8, 128), 0) >> 1)
    for side in range(2):
        blocks = []
        for t in range(2):
            for i in range(2):
                for tile in range(4):
                    at = pl.ds(32 + 8 * tile + 4 * t + 2 * i + side, 1)
                    piece = jnp.where(own[i] == 1, patches[0, at], patches_in[at])
                    blocks.append(jnp.where(stripe, jnp.broadcast_to(piece, (8, 128)), 0.0))
        hi, lo = halves(jnp.concatenate(blocks, axis=0))
        bound += mm(hi, bw[1 + side]) + mm(lo, bw[1 + side])
    x_faces = jnp.concatenate([mixed] * 4, axis=0)
    x_faces = jnp.where(same_group & (wide_lane < 64), x_faces, 0.0)
    hi, lo = halves(x_faces)
    spread = mm(hi, bw[3]) + mm(lo, bw[3])
    fits = (iota((128, 1024), 0) & 15) == (iota((128, 1024), 1) >> 6)
    spread = jnp.where(fits, spread, 0.0)
    kk, rr = iota((128, 128), 1), iota((128, 128), 0)
    lift = jnp.where((kk >> 5) == (rr >> 5), edge((kk >> 4) & 1, rr & 31), 0.0).astype(BF)
    hi, lo = halves(spread)
    bound += mm(lift, hi) + mm(lift, lo)
    bound = bound * (1.0 / 3.0)
    b_old = bound[0:64]
    b_diff = bound[64:128] - b_old

    pair = jnp.where((iota((32, 64), 1) >> 1) == iota((32, 64), 0), 0.125, 0.0).astype(BF)
    sent = []

    def finish(c, values):
        fine_out[c] = values.reshape(2, 32, 1024)
        hi, lo = halves(values)
        flat = mm(hi, mw[...]) + mm(lo, mw[...])
        hi, lo = halves(flat)
        means[c] = mm(pair, hi) + mm(pair, lo)
        back = remote(means.at[c], means_in.at[c], 5 + c, left)
        back.start()
        sent.append(back)

    for step in range(2):
        r = 0.5 * step
        if step == 1:
            first = inside(f)
            second = inside(f + (h / 2) * p)
        one = first + (b_old + r * b_diff)
        mid = b_old + (r + 0.25) * b_diff
        two = second + mid
        three = inside(f + (h / 2) * p + (h * h / 4) * one) + mid
        new = f + h * p + (h * h / 6) * (one + two + three)
        if step == 1:
            finish(0, new)
        four = inside(f + h * p + (h * h / 2) * two) + (b_old + (r + 0.5) * b_diff)
        f = new
        p = p + (h / 6) * (one + 2.0 * two + 2.0 * three + four)
    finish(1, p)

    eye = (iota((8, 128), 1) >> 4) == iota((8, 128), 0)
    z_lane = iota((16, 16, 256), 2)

    new_field.wait()
    into = (coarse_out.at[0], coarse_out.at[1])

    def insert(ref, c, i, keep, y, z):
        values = ref[c, pl.ds(16 * i, 16)]
        blocks = []
        for x in range(16):
            for tile in range(2):
                piece = values[x : x + 1, 128 * tile : 128 * tile + 128]
                blocks.append(jnp.where(eye, jnp.broadcast_to(piece, (8, 128)), 0.0))
        hi, lo = halves(jnp.concatenate(blocks, axis=0))
        place = jnp.where((iota((128, 256), 0) & 15) + z == iota((128, 256), 1), 1.0, 0.0).astype(BF)
        block = (mm(hi, place) + mm(lo, place)).reshape(16, 16, 256)
        for half in range(2):
            chosen = jnp.where(y == 16 * half, keep, 0)
            here = jnp.where((z_lane >> 4) == (z >> 4), chosen, 0) == 1
            rows = pl.ds(16 * half, 16)
            into[c][:, rows] = jnp.where(here, block, into[c][:, rows])

    for c in range(2):
        for i in range(2):
            insert(means, c, i, *corner[i])
    for c in range(2):
        sent[c].wait()
        for i in range(2):
            insert(means_in, c, i, *corner[2 + i])


def shards(devices, state, fine_state, box_list, plan):
    boxes = box_list.T
    cells, ny, nz = state.shape[1:]

    def slab(layers):
        return pltpu.VMEM((layers, ny, nz), F32)

    hbm_spec = pl.BlockSpec(memory_space=pltpu.HBM)

    def body(*refs):
        kernel(devices, *refs)

    vmem_spec = pl.BlockSpec(memory_space=pltpu.VMEM)
    return pl.pallas_call(
        body,
        out_shape=(
            pltpu.VMEM(state.shape, F32),
            pltpu.VMEM(fine_state.shape, F32),
        ),
        in_specs=[hbm_spec, hbm_spec, hbm_spec, hbm_spec],
        out_specs=(vmem_spec, vmem_spec),
        scratch_shapes=[
            slab(cells + 10), slab(cells + 8),
            slab(cells + 8), slab(cells + 6), slab(cells + 4),
            slab(cells + 6), slab(cells + 4), slab(cells + 2),
            pltpu.VMEM(fine_state.shape, F32),
            pltpu.VMEM((2, 48, 1024), F32),
            pltpu.VMEM((2, 64, 128), F32), pltpu.VMEM((64, 128), F32),
            pltpu.VMEM((2, 32, 256), F32), pltpu.VMEM((2, 32, 256), F32),
            pltpu.VMEM((256, 256), BF), pltpu.VMEM((512, 256), BF),
            pltpu.VMEM((4, 128, 1024), BF), pltpu.VMEM((1024, 256), BF),
            pltpu.SMEM(boxes.shape, jnp.int32), pltpu.SMEM(plan.shape, jnp.int32),
            pltpu.SemaphoreType.DMA((5,)),
            pltpu.SemaphoreType.DMA((7,)),
            pltpu.SemaphoreType.DMA((7,)),
        ],
        compiler_params=pltpu.CompilerParams(
            collective_id=0, has_side_effects=True, vmem_limit_bytes=VMEM_LIMIT
        ),
        cost_estimate=pl.CostEstimate(flops=10**9, bytes_accessed=3 * 2**20, transcendentals=0),
        name="refined_step",
    )(state, fine_state, boxes, plan)


def solution(mesh):
    devices = mesh.shape["gx"]

    def local(*args):
        return shards(devices, *args)

    return jax.shard_map(
        local,
        mesh=mesh,
        in_specs=(
            P(None, ("ens", "gx"), None, None),
            P(None, ("ens", "gx"), None, None),
            P("ens", None),
            P("ens"),
        ),
        out_specs=(P(None, ("ens", "gx"), None, None), P(None, ("ens", "gx"), None, None)),
        check_vma=False,
    )
```

```python
import jax
import jax.numpy as jnp
from jax import lax
from jax.experimental import pallas as pl
from jax.experimental.pallas import tpu as pltpu
from jax.sharding import PartitionSpec as P

FB = 32
BOX_DEV = 2
VMEM_LIMIT = 62 * 1024 * 1024
MESH = pl.DeviceIdType.MESH
BF = jnp.bfloat16
F32 = jnp.float32


def iota(shape, dim):
    return lax.broadcasted_iota(jnp.int32, shape, dim)


def halves(a):
    hi = a.astype(BF)
    lo = (a - hi.astype(F32)).astype(BF)
    return hi, lo


def mm(a, b):
    return jnp.dot(a, b, preferred_element_type=F32)


def mm_nt(a, b):
    return lax.dot_general(a, b, (((1,), (1,)), ((), ())), preferred_element_type=F32)


def star(d):
    d = jnp.abs(d)
    return jnp.where(d == 1, 16.0, jnp.where(d == 2, -1.0, 0.0))


def edge(side, j):
    d = jnp.where(side == 0, j, 31 - j)
    return jnp.where(d == 0, 15.0, jnp.where(d == 1, -1.0, 0.0))


def coarse_weights():
    k, j = iota((256, 256), 0), iota((256, 256), 1)
    d = (j - k) & 255
    d = jnp.minimum(d, 256 - d)
    return star(d).astype(BF)


def fine_weights():
    k, j = iota((256, 256), 0), iota((256, 256), 1)
    jy, jz = j >> 5, j & 31
    ky, kz = k >> 5, k & 31
    inner = jnp.where(ky == jy, star(kz - jz), 0.0) + jnp.where(kz == jz, star(ky - jy), 0.0)
    far = jnp.where(k < 128, ky - 4, ky + 4)
    outer = jnp.where(kz == jz, star(far - jy), 0.0)
    return inner.astype(BF), outer.astype(BF)


def boundary_weights():
    k, j = iota((128, 1024), 0), iota((128, 1024), 1)
    y, z = j >> 5, j & 31
    wy = jnp.where((k & 15) == (z >> 1), edge(k >> 6, y), 0.0).astype(BF)
    wzl = jnp.where((k & 31) == (y >> 1), edge(0, z), 0.0).astype(BF)
    wzh = jnp.where((k & 31) == (y >> 1), edge(1, z), 0.0).astype(BF)
    wx = jnp.where((k & 15) == (z >> 1), 1.0, 0.0).astype(BF)
    return wy, wzl, wzh, wx


def mean_weights():
    k, j = iota((1024, 256), 0), iota((1024, 256), 1)
    return jnp.where(((k >> 6) == (j >> 4)) & (((k & 31) >> 1) == (j & 15)), 1.0, 0.0).astype(BF)


def roll(a, shift, axis):
    return pltpu.roll(a, shift % a.shape[axis], axis)


def kernel(
    devices,
    state, fine, boxes_hbm, plan_hbm,
    coarse_out, fine_out,
    fe, pe, f2, f3, f4, k1, k2, nf,
    q, pad, patches, patches_in, means, means_in, cz, fw, bw, mw, boxes, plan,
    local_sem, send_sem, recv_sem,
):
    me = lax.axis_index("gx")
    right, left = lax.rem(me + 1, devices), lax.rem(me + devices - 1, devices)
    cells = state.shape[1]

    barrier = pltpu.get_barrier_semaphore()
    for neighbour in (left, right):
        pl.semaphore_signal(barrier, inc=1, device_id={"gx": neighbour}, device_id_type=MESH)
    loads = [
        pltpu.make_async_copy(state.at[0], fe.at[pl.ds(5, cells)], local_sem.at[0]),
        pltpu.make_async_copy(state.at[1], pe.at[pl.ds(4, cells)], local_sem.at[1]),
        pltpu.make_async_copy(fine, q, local_sem.at[2]),
        pltpu.make_async_copy(boxes_hbm, boxes, local_sem.at[3]),
        pltpu.make_async_copy(plan_hbm, plan, local_sem.at[4]),
    ]
    for load in loads:
        load.start()

    pl.semaphore_wait(barrier, 2)

    def remote(src, dst, number, target):
        return pltpu.make_async_remote_copy(
            src_ref=src, dst_ref=dst, send_sem=send_sem.at[number], recv_sem=recv_sem.at[number],
            device_id={"gx": target}, device_id_type=MESH,
        )

    halo = [
        remote(state.at[0, pl.ds(cells - 5, 5)], fe.at[pl.ds(0, 5)], 0, right),
        remote(state.at[0, pl.ds(0, 5)], fe.at[pl.ds(cells + 5, 5)], 1, left),
        remote(state.at[1, pl.ds(cells - 4, 4)], pe.at[pl.ds(0, 4)], 2, right),
        remote(state.at[1, pl.ds(0, 4)], pe.at[pl.ds(cells + 4, 4)], 3, left),
    ]
    for copy in halo:
        copy.start()

    cz[...] = coarse_weights()
    inner, outer = fine_weights()
    fw[0:256] = inner
    fw[256:512] = outer
    wy, wzl, wzh, wx = boundary_weights()
    bw[0] = wy
    bw[1] = wzl
    bw[2] = wzh
    bw[3] = wx
    mw[...] = mean_weights()
    zeros8 = jnp.zeros((8, 1024), F32)
    for i in range(2):
        pad[i, 0:8] = zeros8
        pad[i, 40:48] = zeros8

    loads[3].wait()
    loads[4].wait()
    corner = []
    for dest in range(2):
        holder = me if dest == 0 else right
        for i in range(2):
            number = plan[holder * BOX_DEV + i]
            x, y, z = boxes[0, number], boxes[1, number], boxes[2, number]
            corner.append((jnp.where(lax.div(x, jnp.int32(cells)) == me, 1, 0), y, z))

    def pick(index, values):
        out = values[-1]
        for number in range(len(values) - 2, -1, -1):
            out = jnp.where(index == number, values[number], out)
        return out

    def force(ref, base, start, n):
        at = start - base
        centre = ref[pl.ds(at, n)]
        near = ref[pl.ds(at - 1, n)] + ref[pl.ds(at + 1, n)]
        far = ref[pl.ds(at - 2, n)] + ref[pl.ds(at + 2, n)]
        near += roll(centre, 1, 1) + roll(centre, -1, 1)
        far += roll(centre, 2, 1) + roll(centre, -2, 1)
        hi, lo = halves(centre.reshape(n * 32, 256))
        along_z = (mm(hi, cz[...]) + mm(lo, cz[...])).reshape(n, 32, 256)
        lap = (16.0 * near - far + along_z - 90.0 * centre) * (1.0 / 12.0)
        return lap + centre * (centre * centre - 1.0)

    def fill_f2(start, n):
        f2[pl.ds(start + 4, n)] = fe[pl.ds(start + 5, n)] + 0.25 * pe[pl.ds(start + 4, n)]

    def stage1(start, n):
        slope = force(fe, -5, start, n)
        k1[pl.ds(start + 3, n)] = slope

    def fill_f3(start, n):
        f3[pl.ds(start + 3, n)] = f2[pl.ds(start + 4, n)] + 0.0625 * k1[pl.ds(start + 3, n)]

    def stage2(start, n):
        slope = force(f2, -4, start, n)
        k2[pl.ds(start + 2, n)] = slope
        f4[pl.ds(start + 2, n)] = fe[pl.ds(start + 5, n)] + 0.5 * pe[pl.ds(start + 4, n)] + 0.125 * slope

    def stage3(start, n):
        slope = force(f3, -3, start, n)
        one, two = k1[pl.ds(start + 3, n)], k2[pl.ds(start + 2, n)]
        nf[pl.ds(start + 1, n)] = (
            fe[pl.ds(start + 5, n)] + 0.5 * pe[pl.ds(start + 4, n)] + (1.0 / 24.0) * (one + two + slope)
        )
        k2[pl.ds(start + 2, n)] = one + 2.0 * two + 2.0 * slope

    def stage4(start, n):
        slope = force(f4, -2, start, n)
        coarse_out[1, pl.ds(start, n)] = pe[pl.ds(start + 4, n)] + (1.0 / 12.0) * (k2[pl.ds(start + 2, n)] + slope)

    loads[0].wait()
    loads[1].wait()
    for s in range(0, 16, 4):
        fill_f2(s, 4)
    for s in range(2, 14, 4):
        stage1(s, 4)
        fill_f3(s, 4)
        stage2(s, 4)
    stage3(4, 4)
    stage3(8, 4)
    loads[2].wait()

    def inside(f):
        for i in range(2):
            pad[i, 8:40] = f[32 * i : 32 * i + 32]
        hi, lo = halves(f)
        none = jnp.zeros((64, 128), BF)

        def gathered(a):
            mid = jnp.concatenate([a[:, 256 * t : 256 * t + 256] for t in range(4)], axis=0)
            before = [none] + [a[:, 256 * t - 128 : 256 * t] for t in range(1, 4)]
            after = [a[:, 256 * t + 256 : 256 * t + 384] for t in range(3)] + [none]
            beside = jnp.concatenate(
                [jnp.concatenate(before, axis=0), jnp.concatenate(after, axis=0)], axis=1
            )
            return jnp.concatenate([mid, beside], axis=1)

        weights = fw[...]
        out = mm(gathered(hi), weights) + mm(gathered(lo), weights)
        along = jnp.concatenate([out[64 * t : 64 * t + 64] for t in range(4)], axis=1)

        def shifted(d):
            return jnp.concatenate([pad[i, 8 + d : 40 + d] for i in range(2)], axis=0)

        lap = 16.0 * (shifted(1) + shifted(-1)) - (shifted(2) + shifted(-2)) + along - 90.0 * f
        return lap * (1.0 / 3.0) + f * (f * f - 1.0)

    h = 0.25
    f = q[0].reshape(64, 1024)
    p = q[1].reshape(64, 1024)
    first = inside(f)
    second = inside(f + (h / 2) * p)

    lane = iota((1, 128), 1)
    group = ((lane >> 6) << 1) + ((lane >> 4) & 1)
    lane_y = pick(group, [c[1] for c in corner])
    lane_z = pick(group, [c[2] for c in corner]) + (lane & 15)
    k = iota((256, 128), 0)
    hit = jnp.where(k == lane_z, 1.0, 0.0)
    rows8 = iota((8, 1), 0)
    row_box = rows8 >> 1
    row_y = pick(row_box, [c[1] for c in corner])
    row_z = pick(row_box, [c[2] for c in corner])
    row_z = jnp.where((rows8 & 1) == 0, row_z + 255, row_z + 16) & 255
    side_hit = jnp.where(iota((8, 256), 1) == row_z, 1.0, 0.0).astype(BF)
    def extract(t, ref, base):
        body = ref[pl.ds(base + 1, cells)]
        rows = jnp.concatenate(
            [ref[base], ref[base + cells + 1], body[:, 31], body[:, 15], body[:, 16], body[:, 0]], axis=0
        )
        hi, lo = halves(rows)
        weight = jnp.where(((iota((256, 128), 1) >> 5) & 1) == t, hit, 0.0).astype(BF)
        part = mm(hi, weight) + mm(lo, weight)
        hi, lo = halves(body.reshape(cells * 32, 256))
        side = mm_nt(side_hit, hi) + mm_nt(side_hit, lo)
        side = jnp.where(jnp.broadcast_to(row_y, (8, 512)) == 0, side, roll(side, -16, 1))
        for dest in range(2):
            for tile in range(4):
                patches[dest, pl.ds(32 + 8 * tile + 4 * t, 4)] = side[
                    4 * dest : 4 * dest + 4, 128 * tile : 128 * tile + 128
                ]
        return part

    for copy in halo[:2]:
        copy.wait()
    for s in (-3, 14):
        stage1(s, 5)
    raw = extract(0, fe, 4)
    for copy in halo[2:]:
        copy.wait()
    for s in (-4, 16):
        fill_f2(s, 4)
    for s in (-3, 14):
        fill_f3(s, 5)
    for s in (-2, 14):
        stage2(s, 4)
    for s in (-1, 12):
        stage3(s, 5)

    raw += extract(1, nf, 0)
    low = jnp.broadcast_to(lane_y, (16, 128)) == 0
    x_part = jnp.concatenate(
        [jnp.where(low, raw[0:16], raw[16:32]), jnp.where(low, raw[32:48], raw[48:64])], axis=0
    )
    y_part = jnp.concatenate(
        [jnp.where(low, raw[64:80], raw[80:96]), jnp.where(low, raw[96:112], raw[112:128])], axis=0
    )
    first_half = iota((32, 128), 1) < 64
    patches[0, 0:32] = jnp.where(first_half, x_part, roll(y_part, 64, 1))
    patches[1, 0:32] = jnp.where(first_half, roll(x_part, 64, 1), y_part)
    patch = [remote(patches.at[1], patches_in, 4, right)]
    for copy in patch:
        copy.start()

    new_field = pltpu.make_async_copy(nf.at[pl.ds(1, cells)], coarse_out.at[0], local_sem.at[0])
    new_field.start()
    for s in range(0, 16, 4):
        stage4(s, 4)

    for copy in patch:
        copy.wait()
    own = [c[0] for c in corner[:2]]
    lane_own = pick((lane >> 4) & 1, own)
    mixed = jnp.where(jnp.broadcast_to(lane_own, (32, 128)) == 1, patches[0, 0:32], patches_in[0:32])
    wide_lane = iota((128, 128), 1)
    same_group = ((wide_lane >> 4) & 3) == (iota((128, 128), 0) >> 5)
    y_faces = jnp.where(iota((16, 128), 1) < 64, roll(mixed[0:16], 64, 1), mixed[16:32])
    up = jnp.where(((iota((128, 16), 0) & 31) >> 1) == iota((128, 16), 1), 1.0, 0.0).astype(BF)
    hi, lo = halves(y_faces)
    wide = mm(up, hi) + mm(up, lo)
    wide = jnp.where(same_group, wide, 0.0)
    hi, lo = halves(wide)
    bound = mm(hi, bw[0]) + mm(lo, bw[0])
    stripe = (iota((8, 128), 1) >> 5) == (iota((8, 128), 0) >> 1)
    for side in range(2):
        blocks = []
        for t in range(2):
            for i in range(2):
                for tile in range(4):
                    at = pl.ds(32 + 8 * tile + 4 * t + 2 * i + side, 1)
                    piece = jnp.where(own[i] == 1, patches[0, at], patches_in[at])
                    blocks.append(jnp.where(stripe, jnp.broadcast_to(piece, (8, 128)), 0.0))
        hi, lo = halves(jnp.concatenate(blocks, axis=0))
        bound += mm(hi, bw[1 + side]) + mm(lo, bw[1 + side])
    x_faces = jnp.concatenate([mixed] * 4, axis=0)
    x_faces = jnp.where(same_group & (wide_lane < 64), x_faces, 0.0)
    hi, lo = halves(x_faces)
    spread = mm(hi, bw[3]) + mm(lo, bw[3])
    fits = (iota((128, 1024), 0) & 15) == (iota((128, 1024), 1) >> 6)
    spread = jnp.where(fits, spread, 0.0)
    kk, rr = iota((128, 128), 1), iota((128, 128), 0)
    lift = jnp.where((kk >> 5) == (rr >> 5), edge((kk >> 4) & 1, rr & 31), 0.0).astype(BF)
    hi, lo = halves(spread)
    bound += mm(lift, hi) + mm(lift, lo)
    bound = bound * (1.0 / 3.0)
    b_old = bound[0:64]
    b_diff = bound[64:128] - b_old

    pair = jnp.where((iota((32, 64), 1) >> 1) == iota((32, 64), 0), 0.125, 0.0).astype(BF)
    sent = []

    def finish(c, values):
        fine_out[c] = values.reshape(2, 32, 1024)
        hi, lo = halves(values)
        flat = mm(hi, mw[...]) + mm(lo, mw[...])
        hi, lo = halves(flat)
        means[c] = mm(pair, hi) + mm(pair, lo)
        back = remote(means.at[c], means_in.at[c], 5 + c, left)
        back.start()
        sent.append(back)

    for step in range(2):
        r = 0.5 * step
        if step == 1:
            first = inside(f)
            second = inside(f + (h / 2) * p)
        one = first + (b_old + r * b_diff)
        mid = b_old + (r + 0.25) * b_diff
        two = second + mid
        three = inside(f + (h / 2) * p + (h * h / 4) * one) + mid
        new = f + h * p + (h * h / 6) * (one + two + three)
        if step == 1:
            finish(0, new)
        four = inside(f + h * p + (h * h / 2) * two) + (b_old + (r + 0.5) * b_diff)
        f = new
        p = p + (h / 6) * (one + 2.0 * two + 2.0 * three + four)
    finish(1, p)

    eye = (iota((8, 128), 1) >> 4) == iota((8, 128), 0)
    z_lane = iota((16, 16, 256), 2)

    new_field.wait()
    into = (coarse_out.at[0], coarse_out.at[1])

    def insert(ref, c, i, keep, y, z):
        values = ref[c, pl.ds(16 * i, 16)]
        blocks = []
        for x in range(16):
            for tile in range(2):
                piece = values[x : x + 1, 128 * tile : 128 * tile + 128]
                blocks.append(jnp.where(eye, jnp.broadcast_to(piece, (8, 128)), 0.0))
        hi, lo = halves(jnp.concatenate(blocks, axis=0))
        place = jnp.where((iota((128, 256), 0) & 15) + z == iota((128, 256), 1), 1.0, 0.0).astype(BF)
        block = (mm(hi, place) + mm(lo, place)).reshape(16, 16, 256)
        for half in range(2):
            chosen = jnp.where(y == 16 * half, keep, 0)
            here = jnp.where((z_lane >> 4) == (z >> 4), chosen, 0) == 1
            rows = pl.ds(16 * half, 16)
            into[c][:, rows] = jnp.where(here, block, into[c][:, rows])

    for c in range(2):
        for i in range(2):
            insert(means, c, i, *corner[i])
    for c in range(2):
        sent[c].wait()
        for i in range(2):
            insert(means_in, c, i, *corner[2 + i])


def shards(devices, state, fine_state, box_list, plan):
    boxes = box_list.T
    cells, ny, nz = state.shape[1:]

    def slab(layers):
        return pltpu.VMEM((layers, ny, nz), F32)

    hbm_spec = pl.BlockSpec(memory_space=pltpu.HBM)

    def body(*refs):
        kernel(devices, *refs)

    vmem_spec = pl.BlockSpec(memory_space=pltpu.VMEM)
    return pl.pallas_call(
        body,
        out_shape=(
            pltpu.VMEM(state.shape, F32),
            pltpu.VMEM(fine_state.shape, F32),
        ),
        in_specs=[hbm_spec, hbm_spec, hbm_spec, hbm_spec],
        out_specs=(vmem_spec, vmem_spec),
        scratch_shapes=[
            slab(cells + 10), slab(cells + 8),
            slab(cells + 8), slab(cells + 6), slab(cells + 4),
            slab(cells + 6), slab(cells + 4), slab(cells + 2),
            pltpu.VMEM(fine_state.shape, F32),
            pltpu.VMEM((2, 48, 1024), F32),
            pltpu.VMEM((2, 64, 128), F32), pltpu.VMEM((64, 128), F32),
            pltpu.VMEM((2, 32, 256), F32), pltpu.VMEM((2, 32, 256), F32),
            pltpu.VMEM((256, 256), BF), pltpu.VMEM((512, 256), BF),
            pltpu.VMEM((4, 128, 1024), BF), pltpu.VMEM((1024, 256), BF),
            pltpu.SMEM(boxes.shape, jnp.int32), pltpu.SMEM(plan.shape, jnp.int32),
            pltpu.SemaphoreType.DMA((5,)),
            pltpu.SemaphoreType.DMA((7,)),
            pltpu.SemaphoreType.DMA((7,)),
        ],
        compiler_params=pltpu.CompilerParams(
            collective_id=0, has_side_effects=True, vmem_limit_bytes=VMEM_LIMIT
        ),
        cost_estimate=pl.CostEstimate(flops=10**9, bytes_accessed=3 * 2**20, transcendentals=0),
        name="refined_step",
    )(state, fine_state, boxes, plan)


def solution(mesh):
    devices = mesh.shape["gx"]

    def local(*args):
        return shards(devices, *args)

    return jax.shard_map(
        local,
        mesh=mesh,
        in_specs=(
            P(None, ("ens", "gx"), None, None),
            P(None, ("ens", "gx"), None, None),
            P("ens", None),
            P("ens"),
        ),
        out_specs=(P(None, ("ens", "gx"), None, None), P(None, ("ens", "gx"), None, None)),
        check_vma=False,
    )
```
